32 devices in a mesh: seq: 16 (over z, y, x), tp: 2 (over core).
Axes of the slice: x: 2, y: 2, z: 4, core: 2. Of those that a mesh axis runs over, the one named last changes fastest.
Arguments:
- latent: bfloat16 [4096, 5120], P('seq', 'tp'), may hold values from -12 to 12
- pose_rows: bfloat16 [4096, 256], P('seq'), may hold values from -6 to 6
- dest_device: int32 [4096, 1], P('seq'), may hold values from 0 to 15; in each aligned block of 256 rows (0 to 255, 256 to 511, ...) at most 32 rows name the same one
- dest_slot: int32 [4096], P('seq'), may hold values from 0 to 255
- w_section1: bfloat16 [16, 32], replicated, may hold values from -1.5 to 1.5
- w_section2: bfloat16 [128, 128], replicated, may hold values from -0.5 to 0.5
- w_section3: bfloat16 [512, 5120], P(None, 'tp'), may hold values from -0.25 to 0.25
- shift_mod: float32 [5120], P('tp'), may hold values from -3 to 3
- scale_mod: float32 [5120], P('tp'), may hold values from -0.5 to 0.5
- w_query: bfloat16 [5120, 5120], P('seq', 'tp'), may hold values from -0.078125 to 0.078125
- bias_query: float32 [5120], P('tp'), may hold values from -3 to 3
- gain_query: float32 [5120], P('tp'), may hold values from 0.25 to 1.75
- cotangent: bfloat16 [4096, 5120], P('seq', 'tp'), may hold values from -16 to 16
Outputs:
- normed_query: bfloat16 [4096, 5120], P('seq', 'tp')
- section_three_grad: float32 [512, 5120], P('seq', 'tp')
- section_two_grad: float32 [128, 128], replicated
- section_one_grad: float32 [16, 32], replicated
The draws below stay inside these ranges and needn't reach their ends.
Inputs may be any that keep to these rules, and one draw needn't show every extreme that they name: `dest_device`: among the rows of one device no index of seq appears more than 32 times, and some index appears exactly 32 times among some device's rows.
All inputs are finite; a program needn't handle non-finite values.
Results may differ from the reference program's by a relative error of at most 0.02.
Values may be sent and summed in bfloat16 or wider, within the bound.
A program may use at most 128 MiB of HBM per device.

```python
import math
import jax
import jax.numpy as jnp
import numpy as np
from jax import lax

D = 5120
C1 = 32
C2 = 128
TOK_DEV = 256
TOKENS = 4096
ROWS = 4096
QW = 5120
CAP = 32
N_SEQ = 16
N_TP = 2


def draw_latent(key, part):
    key_base, key_col = jax.random.split(jax.random.fold_in(key, 11), 2)
    column = jnp.exp(math.log(0.3) + jax.random.uniform(key_col, (1, D), jnp.float32) * math.log(10.0))
    base = jax.random.normal(key_base, (TOKENS, D), jnp.float32)
    base = jnp.clip(base, -4.0, 4.0)
    return (base * column).astype(jnp.bfloat16)


def draw_cotangent(key, part):
    key_base = jax.random.fold_in(key, 23)
    place = jnp.arange(TOKENS, dtype=jnp.float32)[:, None] / max(TOKENS - 1, 1)
    base = jnp.clip(jax.random.normal(key_base, (TOKENS, QW), jnp.float32), -4.0, 4.0)
    rising = 1.0 + 2.0 * place
    return (base * rising * (1.0 / math.sqrt(TOKENS))).astype(jnp.bfloat16)


def with_ends(values, rng, least, top_value):
    spot = [jax.random.randint(jax.random.fold_in(rng, axis), (), 0, length) for axis, length in enumerate(values.shape)]
    widest = values.shape.index(max(values.shape))
    beside = spot[:widest] + [(spot[widest] + 1) % values.shape[widest]] + spot[widest + 1:]
    return values.at[tuple(spot)].set(least).at[tuple(beside)].set(top_value)


def levels(stream_key, extent, shards, least, largest):
    factor_of, own = 1.0, jax.random.fold_in(stream_key, 6)
    for dim, parts in shards:
        heights = jnp.exp(jax.random.uniform(jax.random.fold_in(own, dim), (parts,), jnp.float32, least / len(shards), largest / len(shards)))
        factor_of = factor_of * jnp.repeat(heights, extent[dim] // parts).reshape([-1 if axis == dim else 1 for axis in range(len(extent))])
    return factor_of


def deal_out(stream_key, own, number, rows, number_of, top, bound, lean):
    order = jax.random.permutation(stream_key, number_of)
    crowded, ordinary = load_shares(number_of, rows * top, bound, lean, True), load_shares(number_of, rows * top, bound, lean, False)
    places = jnp.arange(number_of)

    def named(lengths, rotation):
        used = int((lengths > 0).sum())
        fixed = max(1, used // 4)
        moved = fixed + (places - fixed + rotation * (used - fixed)) % max(1, number_of - fixed)
        return jnp.zeros((number_of,), jnp.int32).at[order[jnp.where(places < fixed, places, moved)]].set(jnp.asarray(lengths, jnp.int32))

    lengths = jnp.where(number % 4 == 0, named(crowded, number // 4), named(ordinary, number - number // 4 - 1))
    mixed = jax.random.permutation(jax.random.fold_in(own, 3), number_of)
    giver, taker = mixed[0:number_of // 2 * 2:2], mixed[1:number_of // 2 * 2:2]
    slack = jnp.minimum(lengths[giver] - 1, bound - lengths[taker]) // 2
    slack = jnp.where((giver == order[0]) | (taker == order[0]) | (lengths[taker] == 0), 0, jnp.maximum(slack, 0))
    moved = jax.random.randint(jax.random.fold_in(own, 4), (number_of // 2,), 0, 1 << 20) % (slack + 1)
    lengths = lengths.at[giver].add(-moved).at[taker].add(moved)
    labels = jnp.searchsorted(jnp.cumsum(lengths), jnp.arange(rows * top), side="right").astype(jnp.int32)
    listing = labels.reshape(top, rows).T
    listing = listing[jax.random.permutation(jax.random.fold_in(own, 1), rows)]
    rotation = jax.random.randint(jax.random.fold_in(own, 2), (rows, 1), 0, top)
    return jnp.take_along_axis(listing, (jnp.arange(top)[None, :] + rotation) % top, axis=1)


def load_shares(amount, total, reach, skew, full):
    weights = [(1 << 20) // math.isqrt(standing ** skew) + 1 for standing in range(1, amount + 1)]
    largest = reach if full else min(reach, max(-(-total // amount), total * weights[0] // sum(weights)))
    least = 1 if total - largest >= amount - 1 else 0
    counts, spare = [largest] + [least] * (amount - 1), total - largest - least * (amount - 1)
    while spare > 0:
        free = [i for i in range(1, amount) if counts[i] < largest] or [i for i in range(1, amount) if counts[i] < reach]
        whole, budget = sum([weights[i] for i in free]), spare
        for i in free:
            more = min(reach - counts[i], max(1, budget * weights[i] // whole), spare)
            counts[i] = counts[i] + more
            spare = spare - more
    return np.array(counts)


def scatter_about(stream_key, dims, scale, bound, cuts=(), kind=jnp.bfloat16):
    array = jax.random.normal(stream_key, dims, jnp.float32) * scale
    if len(cuts) > 0:
        array = levels(stream_key, dims, cuts, -0.22, 0.18) * array
    return jnp.clip(array, min=-bound, max=bound).astype(kind)


def setup_inputs(seed: int = 0) -> dict:
    key_list = jax.random.split(jax.random.key(seed), 14)
    latent = draw_latent(jax.random.fold_in(key_list[13], 71), 0)
    pose_rows = scatter_about(key_list[1], (ROWS, 256), 1.5, 6.0, ((0, 16),))
    dest_device_keys = jax.random.split(jax.random.fold_in(key_list[2], 1), ROWS // TOK_DEV)
    dest_device_turns = jax.random.permutation(jax.random.fold_in(key_list[2], 3), ROWS // TOK_DEV)
    dest_device = jax.vmap(lambda own, number: deal_out(jax.random.fold_in(key_list[2], 2), own, number, TOK_DEV, N_SEQ, 1, CAP, 2))(dest_device_keys, dest_device_turns).reshape((ROWS, 1))
    dest_slot = with_ends(jax.random.randint(key_list[3], (ROWS,), 0, TOK_DEV), jax.random.fold_in(key_list[3], 1), 0, TOK_DEV - 1).astype(jnp.int32)
    w_section1 = scatter_about(key_list[4], (16, C1), 16 ** -0.5, 1.5)
    w_section2 = scatter_about(key_list[5], (4 * C1, C2), (4 * C1) ** -0.5, 0.5)
    w_section3 = scatter_about(key_list[6], (4 * C2, D), (4 * C2) ** -0.5, 0.25, ((1, 2),))
    shift_mod = scatter_about(key_list[7], (D,), 0.5, 3.0, ((0, 2),), jnp.float32)
    scale_mod = jnp.clip(jax.random.uniform(key_list[8], (D,), jnp.float32, -0.5, 0.5) * levels(key_list[8], (D,), ((0, 2),), -0.4, 0.0), -0.5, 0.5)
    w_query = scatter_about(key_list[9], (D, QW), D ** -0.5, 0.078125, ((0, 16), (1, 2)))
    bias_query = scatter_about(key_list[10], (QW,), 0.5, 3.0, ((0, 2),), jnp.float32)
    gain_query = jnp.clip(1.0 + 0.15 * jax.random.normal(key_list[11], (QW,), jnp.float32), 0.25, 1.75)
    cotangent = draw_cotangent(jax.random.fold_in(key_list[13], 71), 0)
    return {"latent": latent, "pose_rows": pose_rows, "dest_device": dest_device, "dest_slot": dest_slot, "w_section1": w_section1, "w_section2": w_section2, "w_section3": w_section3, "shift_mod": shift_mod, "scale_mod": scale_mod, "w_query": w_query, "bias_query": bias_query, "gain_query": gain_query, "cotangent": cotangent}


epsilon = 1e-06

def silu_slope(z):
    s = jax.nn.sigmoid(z)
    return s * (1.0 + z * (1.0 - s))

def run_sections(pose, w_one, w_two):
    count = pose.shape[0]
    c_one = w_one.shape[1]
    cells = pose.reshape(count * 16, 16)
    z_one = jnp.dot(cells, w_one, preferred_element_type=jnp.float32)
    feature_one = jax.nn.silu(z_one).astype(jnp.bfloat16)
    stacked_one = feature_one.reshape(count, 2, 2, 2, 2, c_one).transpose(0, 1, 3, 2, 4, 5).reshape(count * 4, 4 * c_one)
    z_two = jnp.dot(stacked_one, w_two, preferred_element_type=jnp.float32)
    stacked_two = jax.nn.silu(z_two).astype(jnp.bfloat16).reshape(count, 4 * w_two.shape[1])
    return (cells, z_one, stacked_one, z_two, stacked_two)

def section_back(cells, z_one, stacked_one, z_two, stacked_grad, w_two):
    quads = z_two.shape[0]
    count = quads // 4
    c_one = z_one.shape[1]
    two_grad = stacked_grad.reshape(quads, -1) * silu_slope(z_two)
    grad_two = lax.dot_general(stacked_one.astype(jnp.float32), two_grad, (((0,), (0,)), ((), ())), precision=lax.Precision.HIGHEST)
    back_one = jnp.dot(two_grad, w_two.astype(jnp.float32).T, precision=lax.Precision.HIGHEST)
    back_one = back_one.reshape(count, 2, 2, 2, 2, c_one).transpose(0, 1, 3, 2, 4, 5).reshape(count * 16, c_one)
    one_grad = back_one * silu_slope(z_one)
    grad_one = lax.dot_general(cells.astype(jnp.float32), one_grad, (((0,), (0,)), ((), ())), precision=lax.Precision.HIGHEST)
    return (grad_two, grad_one)

def reference(latent, pose_rows, dest_device, dest_slot, w_section1, w_section2, w_section3, shift_mod, scale_mod, w_query, bias_query, gain_query, cotangent):
    cells, z_one, stacked_one, z_two, stacked_two = run_sections(pose_rows, w_section1, w_section2)
    pose_tokens = jnp.dot(stacked_two, w_section3, preferred_element_type=jnp.float32).astype(jnp.bfloat16)
    target = (dest_device[:, 0] * TOK_DEV + dest_slot).astype(jnp.int32)
    guidance = jnp.zeros((TOKENS, D), jnp.float32).at[target].add(pose_tokens.astype(jnp.float32))
    summed = latent.astype(jnp.float32) + guidance
    center = lax.optimization_barrier(jnp.mean(summed, axis=1, keepdims=True))
    shifted = summed - center
    spread = lax.optimization_barrier(jnp.mean(shifted * shifted, axis=1, keepdims=True))
    inverse = lax.rsqrt(spread + epsilon)
    normed = shifted * inverse
    modulated = (normed * (1.0 + scale_mod) + shift_mod).astype(jnp.bfloat16)
    query = jnp.dot(modulated, w_query, preferred_element_type=jnp.float32) + bias_query
    rinv = lax.rsqrt(lax.optimization_barrier(jnp.mean(query * query, axis=1, keepdims=True)) + epsilon)
    normed_query = (query * rinv * gain_query).astype(jnp.bfloat16)
    upstream = cotangent.astype(jnp.float32) * gain_query
    along = lax.optimization_barrier(jnp.mean(upstream * query, axis=1, keepdims=True))
    query_grad = (upstream * rinv - query * along * rinv ** 3).astype(jnp.bfloat16)
    block_width = QW // N_TP
    modulated_grad = jnp.zeros((TOKENS, D), jnp.float32)
    for group in range(N_TP):
        lo_col = group * block_width
        term = jnp.dot(query_grad[:, lo_col:lo_col + block_width], w_query[:, lo_col:lo_col + block_width].T, preferred_element_type=jnp.float32)
        modulated_grad = modulated_grad + lax.optimization_barrier(term.astype(jnp.bfloat16)).astype(jnp.float32)
    normed_grad = modulated_grad * (1.0 + scale_mod)
    latent_grad = inverse * (normed_grad - lax.optimization_barrier(jnp.mean(normed_grad, axis=1, keepdims=True)) - normed * lax.optimization_barrier(jnp.mean(normed_grad * normed, axis=1, keepdims=True)))
    latent_grad = latent_grad.astype(jnp.bfloat16)
    row_grad = latent_grad[target]
    section_three_grad = lax.dot_general(stacked_two, row_grad, (((0,), (0,)), ((), ())), preferred_element_type=jnp.float32)
    stacked_grad = jnp.dot(row_grad, w_section3.T, preferred_element_type=jnp.float32)
    section_two_grad, section_one_grad = section_back(cells, z_one, stacked_one, z_two, stacked_grad, w_section2)
    return (normed_query, section_three_grad, section_two_grad, section_one_grad)
```

```python
import jax
import jax.numpy as jnp
import numpy as np
from jax import lax
from jax.sharding import PartitionSpec as P

epsilon = 1e-06
F32, BF16 = jnp.float32, jnp.bfloat16


def silu_slope(z):
    s = jax.nn.sigmoid(z)
    return s * (1.0 + z * (1.0 - s))


def mm(a, b):
    return jnp.dot(a, b, preferred_element_type=F32)


def mm_nt(a, b):
    return lax.dot_general(a, b, (((1,), (1,)), ((), ())), preferred_element_type=F32)


def mm_tn(a, b):
    return lax.dot_general(a, b, (((0,), (0,)), ((), ())), preferred_element_type=F32)


def cell_places():
    table = np.zeros((16, 16), np.float32)
    for i in range(4):
        for j in range(4):
            place = ((i // 2) * 2 + j // 2) * 4 + (i % 2) * 2 + j % 2
            table[4 * i + j, place] = 1.0
    return jnp.asarray(table)


def spread_one(w_one):
    depth, c_one = w_one.shape
    wide = cell_places()[:, None, :, None] * w_one.astype(F32)[None, :, None, :]
    return wide.reshape(16 * depth, 16 * c_one).astype(BF16)


def fold_one(wide, depth, c_one):
    blocks = wide.reshape(16, depth, 16, c_one) * cell_places()[:, None, :, None]
    return jnp.sum(blocks, axis=(0, 2))


def dispatch(pose_rows, dest_device, dest_slot, seq_count):
    count, width = pose_rows.shape
    capacity = max(2, 2 * count // seq_count)
    slots_all = seq_count * capacity
    owner = dest_device[:, 0]
    marks = (owner[:, None] == jnp.arange(seq_count, dtype=jnp.int32)[None, :]).astype(BF16)
    index = jnp.arange(count, dtype=jnp.int32)
    lower = (index[:, None] > index[None, :]).astype(BF16)
    before = mm(lower, marks)
    rank = jnp.sum(before * marks.astype(F32), axis=1).astype(jnp.int32)
    position = owner * capacity + rank
    place = (jnp.arange(slots_all, dtype=jnp.int32)[:, None] == position[None, :]).astype(BF16)
    lane = jnp.arange(128, dtype=jnp.int32)[None, :]
    slot = dest_slot[:, None]
    tail = jnp.where(lane == 0, slot // 128, jnp.where(lane == 1, slot % 128, jnp.where(lane == 2, 1, 0)))
    rows = jnp.concatenate([pose_rows, tail.astype(BF16)], axis=1)
    outgoing = mm(place, rows).astype(BF16)
    incoming = lax.all_to_all(
        outgoing.reshape(seq_count, capacity, width + 128), "seq", split_axis=0, concat_axis=0, tiled=True
    ).reshape(slots_all, width + 128)
    info = incoming[:, width : width + 3].astype(F32)
    slot_recv = (info[:, 0] * 128.0 + info[:, 1]).astype(jnp.int32)
    slot_recv = jnp.where(info[:, 2] > 0.5, slot_recv, -1)
    return incoming[:, :width], slot_recv


def body(
    latent,
    pose_rows,
    dest_device,
    dest_slot,
    w_section1,
    w_section2,
    w_section3,
    shift_mod,
    scale_mod,
    w_query,
    bias_query,
    gain_query,
    cotangent,
):
    tokens = latent.shape[0]
    seq_count = lax.axis_size("seq")
    tp_count = lax.axis_size("tp")
    full_width = latent.shape[1] * tp_count
    query_width = w_query.shape[1] * tp_count
    depth, c_one = w_section1.shape
    c_two = w_section2.shape[1]
    weights_all = lax.all_gather(w_query, "seq", axis=0, tiled=True)
    pose_in, slot_recv = dispatch(pose_rows, dest_device, dest_slot, seq_count)
    w_wide = spread_one(w_section1)
    w_quad = jnp.kron(jnp.eye(4, dtype=BF16), w_section2)
    z_one = mm(pose_in, w_wide)
    stacked_one = jax.nn.silu(z_one).astype(BF16)
    z_two = mm(stacked_one, w_quad)
    stacked_two = jax.nn.silu(z_two).astype(BF16)
    select = (jnp.arange(tokens, dtype=jnp.int32)[:, None] == slot_recv[None, :]).astype(BF16)
    token_two = mm(select, stacked_two).astype(BF16)
    guidance = mm(token_two, w_section3)
    summed = latent.astype(F32) + guidance
    total, squares = lax.psum((jnp.sum(summed, axis=1), jnp.sum(summed * summed, axis=1)), "tp")
    center = total / full_width
    inverse = lax.rsqrt(squares / full_width - center * center + epsilon)[:, None]
    normed = (summed - center[:, None]) * inverse
    modulated = (normed * (1.0 + scale_mod) + shift_mod).astype(BF16)
    whole = lax.all_gather(modulated, "tp", axis=1, tiled=True)
    query = mm(whole, weights_all) + bias_query
    upstream = cotangent.astype(F32) * gain_query
    sum_square, sum_along = lax.psum(
        (jnp.sum(query * query, axis=1), jnp.sum(upstream * query, axis=1)), "tp"
    )
    rinv = lax.rsqrt(sum_square / query_width + epsilon)[:, None]
    normed_query = (query * rinv * gain_query).astype(BF16)
    along = (sum_along / query_width)[:, None]
    query_grad = (upstream * rinv - query * along * rinv**3).astype(BF16)
    partial_grad = mm_nt(query_grad, weights_all)
    modulated_grad = lax.psum_scatter(
        partial_grad.astype(BF16), "tp", scatter_dimension=1, tiled=True
    ).astype(F32)
    normed_grad = modulated_grad * (1.0 + scale_mod)
    grad_total, grad_cross = lax.psum(
        (jnp.sum(normed_grad, axis=1), jnp.sum(normed_grad * normed, axis=1)), "tp"
    )
    latent_grad = inverse * (
        normed_grad
        - (grad_total / full_width)[:, None]
        - normed * (grad_cross / full_width)[:, None]
    )
    latent_grad = latent_grad.astype(BF16)
    section_three_grad = lax.psum_scatter(
        mm_tn(token_two, latent_grad).astype(BF16), "seq", scatter_dimension=0, tiled=True
    ).astype(F32)
    token_grad = mm_nt(latent_grad, w_section3).astype(BF16)
    stacked_grad = mm_tn(select, token_grad)
    two_grad = (stacked_grad * silu_slope(z_two)).astype(BF16)
    wide_two = mm_tn(stacked_one, two_grad)
    grad_two = sum(
        wide_two[4 * c_one * q : 4 * c_one * (q + 1), c_two * q : c_two * (q + 1)] for q in range(4)
    )
    one_grad = (mm_nt(two_grad, w_quad) * silu_slope(z_one)).astype(BF16)
    grad_one = fold_one(mm_tn(pose_in, one_grad), depth, c_one)
    packed = jnp.concatenate([grad_two.reshape(-1), grad_one.reshape(-1)])
    packed = lax.psum(packed, ("seq", "tp"))
    cut = grad_two.size
    return (
        normed_query,
        section_three_grad,
        packed[:cut].reshape(grad_two.shape),
        packed[cut:].reshape(grad_one.shape),
    )


def solution(mesh):
    return jax.shard_map(
        body,
        mesh=mesh,
        in_specs=(
            P("seq", "tp"),
            P("seq", None),
            P("seq", None),
            P("seq"),
            P(),
            P(),
            P(None, "tp"),
            P("tp"),
            P("tp"),
            P("seq", "tp"),
            P("tp"),
            P("tp"),
            P("seq", "tp"),
        ),
        out_specs=(P("seq", "tp"), P("seq", "tp"), P(), P()),
        check_vma=False,
    )
```

```python
import jax
import jax.numpy as jnp
import numpy as np
from jax import lax
from jax.experimental import pallas as pl
from jax.experimental.pallas import tpu as pltpu
from jax.sharding import PartitionSpec as P

MESH = pl.DeviceIdType.MESH

epsilon = 1e-06
F32, BF16 = jnp.float32, jnp.bfloat16


def silu_slope(z):
    s = jax.nn.sigmoid(z)
    return s * (1.0 + z * (1.0 - s))


def mm(a, b):
    return jnp.dot(a, b, preferred_element_type=F32)


def mm_nt(a, b):
    return lax.dot_general(a, b, (((1,), (1,)), ((), ())), preferred_element_type=F32)


def mm_tn(a, b):
    return lax.dot_general(a, b, (((0,), (0,)), ((), ())), preferred_element_type=F32)


def cell_places():
    table = np.zeros((16, 16), np.float32)
    for i in range(4):
        for j in range(4):
            place = ((i // 2) * 2 + j // 2) * 4 + (i % 2) * 2 + j % 2
            table[4 * i + j, place] = 1.0
    return jnp.asarray(table)


def spread_one(w_one):
    depth, c_one = w_one.shape
    wide = cell_places()[:, None, :, None] * w_one.astype(F32)[None, :, None, :]
    return wide.reshape(16 * depth, 16 * c_one).astype(BF16)


def fold_one(wide, depth, c_one):
    blocks = wide.reshape(16, depth, 16, c_one) * cell_places()[:, None, :, None]
    return jnp.sum(blocks, axis=(0, 2))


def dispatch(pose_rows, dest_device, dest_slot, seq_count):
    count, width = pose_rows.shape
    capacity = max(2, 2 * count // seq_count)
    slots_all = seq_count * capacity
    owner = dest_device[:, 0]
    marks = (owner[:, None] == jnp.arange(seq_count, dtype=jnp.int32)[None, :]).astype(BF16)
    index = jnp.arange(count, dtype=jnp.int32)
    lower = (index[:, None] > index[None, :]).astype(BF16)
    before = mm(lower, marks)
    rank = jnp.sum(before * marks.astype(F32), axis=1).astype(jnp.int32)
    position = owner * capacity + rank
    place = (jnp.arange(slots_all, dtype=jnp.int32)[:, None] == position[None, :]).astype(BF16)
    lane = jnp.arange(128, dtype=jnp.int32)[None, :]
    slot = dest_slot[:, None]
    tail = jnp.where(lane == 0, slot // 128, jnp.where(lane == 1, slot % 128, jnp.where(lane == 2, 1, 0)))
    rows = jnp.concatenate([pose_rows, tail.astype(BF16)], axis=1)
    outgoing = mm(place, rows).astype(BF16)
    incoming = lax.all_to_all(
        outgoing.reshape(seq_count, capacity, width + 128), "seq", split_axis=0, concat_axis=0, tiled=True
    ).reshape(slots_all, width + 128)
    info = incoming[:, width : width + 3].astype(F32)
    slot_recv = (info[:, 0] * 128.0 + info[:, 1]).astype(jnp.int32)
    slot_recv = jnp.where(info[:, 2] > 0.5, slot_recv, -1)
    return incoming[:, :width], slot_recv


def place_here():
    me, core = lax.axis_index("seq"), lax.axis_index("tp")
    return me // 4, (me // 2) % 2, me % 2, core


def greet(devices, count):
    barrier = pltpu.get_barrier_semaphore()
    for condition, device in devices:

        def say(device=device):
            pl.semaphore_signal(barrier, inc=1, device_id=device, device_id_type=MESH)

        if condition is None:
            say()
        else:
            pl.when(condition)(say)
    pl.semaphore_wait(barrier, count)


def gather_kernel(w_ref, out_ref, own_sem, up_send, up_recv, down_send, down_recv, send_sem, recv_sem):
    z, y, x, core = place_here()
    half = w_ref.shape[0] // 2
    rows_a, rows_b = pl.ds(0, half), pl.ds(half, half)
    last = 3

    def device(zz, yy, xx):
        return (zz * 4 + yy * 2 + xx, core)

    x_side, y_side = device(z, y, 1 - x), device(z, 1 - y, x)
    above, below = device(jnp.minimum(z + 1, last), y, x), device(jnp.maximum(z - 1, 0), y, x)
    greet(
        [(None, x_side), (None, y_side), (z < last, above), (z > 0, below)],
        2 + (z < last).astype(jnp.int32) + (z > 0).astype(jnp.int32),
    )

    def remote(src, dst, sems, target):
        return pltpu.make_async_remote_copy(
            src_ref=src, dst_ref=dst, send_sem=sems[0], recv_sem=sems[1], device_id=target, device_id_type=MESH
        )

    def line_copy(zz, step, up, src=None):
        block = out_ref.at[zz, y, x]
        send, recv = (up_send, up_recv) if up else (down_send, down_recv)
        return remote(block if src is None else src, block, (send.at[step], recv.at[step]), above if up else below)

    kinds = (
        (y, x, rows_a, True),
        (y, x, rows_b, False),
        (y, x, rows_a, False),
        (y, x, rows_b, True),
        (y, 1 - x, rows_a, False),
        (1 - y, x, rows_b, True),
    )

    def plane_copy(kind, zz, own=False):
        yy, xx, rows, to_x = kinds[kind]
        block = out_ref.at[zz, yy, xx, rows]
        return remote(
            w_ref.at[rows] if own else block,
            block,
            (send_sem.at[kind, zz], recv_sem.at[kind, zz]),
            x_side if to_x else y_side,
        )

    def arrival(kind, zz):
        yy, xx, rows, to_x = kinds[kind]
        yy, xx = (yy, 1 - xx) if to_x else (1 - yy, xx)
        block = out_ref.at[zz, yy, xx, rows]
        return remote(block, block, (send_sem.at[kind, zz], recv_sem.at[kind, zz]), x_side if to_x else y_side)

    def relay(zz):
        arrival(0, zz).wait_recv()
        plane_copy(4, zz).start()
        arrival(1, zz).wait_recv()
        plane_copy(5, zz).start()

    pl.when(z < last)(lambda: line_copy(z, 0, True, w_ref).start())
    pl.when(z > 0)(lambda: line_copy(z, 0, False, w_ref).start())
    for kind in range(4):
        plane_copy(kind, z, True).start()
    own = pltpu.make_async_copy(w_ref, out_ref.at[z, y, x], own_sem)
    own.start()
    for step in range(1, 4):
        for up in (True, False):
            zz = z - step if up else z + step
            came = zz >= 0 if up else zz <= last
            goes_on = jnp.logical_and(came, z < last if up else z > 0)

            def arrive(zz=zz, step=step, up=up):
                line_copy(zz, step - 1, up).wait_recv()

            def pass_on(zz=zz, step=step, up=up):
                line_copy(zz, step, up).start()

            def spread(zz=zz):
                for kind in range(4):
                    plane_copy(kind, zz).start()

            pl.when(came)(arrive)
            if step < 3:
                pl.when(goes_on)(pass_on)
            pl.when(came)(spread)
        if step == 1:
            relay(z)
        else:
            for zz, came in ((z - step + 1, z - step + 1 >= 0), (z + step - 1, z + step - 1 <= last)):
                pl.when(came)(lambda zz=zz: relay(zz))
    for zz, came in ((z - 3, z - 3 >= 0), (z + 3, z + 3 <= last)):
        pl.when(came)(lambda zz=zz: relay(zz))
    own.wait()
    for zz in range(4):
        for kind in range(2, 6):
            arrival(kind, zz).wait_recv()
        for kind in range(6):
            plane_copy(kind, zz).wait_send()
    for step in range(3):
        pl.when(jnp.logical_and(z - step >= 0, z < last))(
            lambda step=step: line_copy(z - step, step, True).wait_send()
        )
        pl.when(jnp.logical_and(z + step <= last, z > 0))(
            lambda step=step: line_copy(z + step, step, False).wait_send()
        )


def gather_weights(w_query):
    depth, columns = w_query.shape
    dma = pltpu.SemaphoreType.DMA
    out = pl.pallas_call(
        gather_kernel,
        out_shape=jax.ShapeDtypeStruct((4, 2, 2, depth, columns), w_query.dtype),
        in_specs=[pl.BlockSpec(memory_space=pl.ANY)],
        out_specs=pl.BlockSpec(memory_space=pl.ANY),
        scratch_shapes=[dma, dma((3,)), dma((3,)), dma((3,)), dma((3,)), dma((6, 4)), dma((6, 4))],
        compiler_params=pltpu.CompilerParams(collective_id=0, has_side_effects=True),
    )(w_query)
    return out.reshape(16 * depth, columns)


def reduce_kernel(
    p_ref, g_ref, out_ref, small_ref, one_a, one_b, sum_a, sum_b, two_a, two_b, line, line_in,
    small, small_in, small_z, send_sem, recv_sem, line_send, line_recv, g_send, g_recv, gz_send, gz_recv,
):
    z, y, x, core = place_here()
    half = p_ref.shape[-1] // 2
    cols_a, cols_b = pl.ds(0, half), pl.ds(half, half)

    def device(zz, yy, xx, cc):
        return (zz * 4 + yy * 2 + xx, cc)

    x_side, y_side, core_side = device(z, y, 1 - x, core), device(z, 1 - y, x, core), device(z, y, x, 1 - core)
    peers = [lax.rem(z + d, 4) for d in (1, 2, 3)]
    greet([(None, t) for t in [x_side, y_side, core_side] + [device(p, y, x, core) for p in peers]], 6)

    def send(src, dst, sems, target):
        copy = pltpu.make_async_remote_copy(
            src_ref=src, dst_ref=dst, send_sem=sems[0], recv_sem=sems[1], device_id=target, device_id_type=MESH
        )
        copy.start()
        return copy

    def sems(i):
        return (send_sem.at[i], recv_sem.at[i])

    def added(a, b):
        return (a.astype(F32) + b.astype(F32)).astype(BF16)

    first_a = send(p_ref.at[:, :, 1 - x, :, cols_a], one_a, sems(0), x_side)
    first_b = send(p_ref.at[:, 1 - y, :, :, cols_b], one_b, sems(1), y_side)
    small[0] = g_ref[...]
    for i, target in enumerate((core_side, x_side, y_side)):
        send(small.at[i], small_in.at[i], (g_send.at[i], g_recv.at[i]), target).wait()
        small[i + 1] = small[i] + small_in[i]
    small_z[z] = small[3]
    g_line = [
        send(small.at[3], small_z.at[z], (gz_send.at[d], gz_recv.at[d]), device(peers[d], y, x, core))
        for d in range(3)
    ]
    first_a.wait()
    for zz in range(4):
        for q in range(2):
            sum_a[zz, q] = added(p_ref[zz, q, x, :, 0:half], one_a[zz, q])
    second_a = send(sum_a.at[:, 1 - y], two_a, sems(2), y_side)
    first_b.wait()
    for zz in range(4):
        for q in range(2):
            sum_b[zz, q] = added(p_ref[zz, y, q, :, half:], one_b[zz, q])
    second_b = send(sum_b.at[:, 1 - x], two_b, sems(3), x_side)
    second_a.wait()
    for zz in range(4):
        line[zz, :, 0:half] = added(sum_a[zz, y], two_a[zz])
    second_b.wait()
    for zz in range(4):
        line[zz, :, half:] = added(sum_b[zz, x], two_b[zz])
    last = [
        send(line.at[peers[d]], line_in.at[d], (line_send.at[d], line_recv.at[d]), device(peers[d], y, x, core))
        for d in range(3)
    ]
    for copy in g_line:
        copy.wait()
    small_ref[...] = (small_z[0] + small_z[1]) + (small_z[2] + small_z[3])
    for copy in last:
        copy.wait()
    total = line[z].astype(F32)
    for d in range(3):
        total = total + line_in[d].astype(F32)
    out_ref[...] = total


def reduce_grads(partial, small):
    rows, columns = partial.shape
    piece, half = rows // 16, columns // 2
    dma = pltpu.SemaphoreType.DMA
    vmem = pl.BlockSpec(memory_space=pltpu.VMEM)
    return pl.pallas_call(
        reduce_kernel,
        out_shape=(jax.ShapeDtypeStruct((piece, columns), F32), jax.ShapeDtypeStruct(small.shape, F32)),
        in_specs=[vmem, vmem],
        out_specs=(vmem, vmem),
        scratch_shapes=[pltpu.VMEM((4, 2, piece, half), BF16)] * 4
        + [pltpu.VMEM((4, piece, half), BF16)] * 2
        + [pltpu.VMEM((4, piece, columns), BF16), pltpu.VMEM((3, piece, columns), BF16)]
        + [pltpu.VMEM((4,) + small.shape, F32), pltpu.VMEM((3,) + small.shape, F32), pltpu.VMEM((4,) + small.shape, F32)]
        + [dma((4,)), dma((4,)), dma((3,)), dma((3,)), dma((3,)), dma((3,)), dma((3,)), dma((3,))],
        compiler_params=pltpu.CompilerParams(collective_id=1, has_side_effects=True, vmem_limit_bytes=32 << 20),
    )(partial.reshape(4, 2, 2, piece, columns), small)


def body(
    latent,
    pose_rows,
    dest_device,
    dest_slot,
    w_section1,
    w_section2,
    w_section3,
    shift_mod,
    scale_mod,
    w_query,
    bias_query,
    gain_query,
    cotangent,
):
    tokens = latent.shape[0]
    seq_count = lax.axis_size("seq")
    tp_count = lax.axis_size("tp")
    full_width = latent.shape[1] * tp_count
    query_width = w_query.shape[1] * tp_count
    depth, c_one = w_section1.shape
    c_two = w_section2.shape[1]
    chips = seq_count == 16 and tp_count == 2
    if chips:
        weights_all = gather_weights(w_query)
    else:
        weights_all = lax.all_gather(w_query, "seq", axis=0, tiled=True)
    pose_in, slot_recv = dispatch(pose_rows, dest_device, dest_slot, seq_count)
    w_wide = spread_one(w_section1)
    w_quad = jnp.kron(jnp.eye(4, dtype=BF16), w_section2)
    z_one = mm(pose_in, w_wide)
    stacked_one = jax.nn.silu(z_one).astype(BF16)
    z_two = mm(stacked_one, w_quad)
    stacked_two = jax.nn.silu(z_two).astype(BF16)
    select = (jnp.arange(tokens, dtype=jnp.int32)[:, None] == slot_recv[None, :]).astype(BF16)
    token_two = mm(select, stacked_two).astype(BF16)
    guidance = mm(token_two, w_section3)
    summed = latent.astype(F32) + guidance
    total, squares = lax.psum((jnp.sum(summed, axis=1), jnp.sum(summed * summed, axis=1)), "tp")
    center = total / full_width
    inverse = lax.rsqrt(squares / full_width - center * center + epsilon)[:, None]
    normed = (summed - center[:, None]) * inverse
    modulated = (normed * (1.0 + scale_mod) + shift_mod).astype(BF16)
    whole = lax.all_gather(modulated, "tp", axis=1, tiled=True)
    query = mm(whole, weights_all) + bias_query
    upstream = cotangent.astype(F32) * gain_query
    sum_square, sum_along = lax.psum(
        (jnp.sum(query * query, axis=1), jnp.sum(upstream * query, axis=1)), "tp"
    )
    rinv = lax.rsqrt(sum_square / query_width + epsilon)[:, None]
    normed_query = (query * rinv * gain_query).astype(BF16)
    along = (sum_along / query_width)[:, None]
    query_grad = (upstream * rinv - query * along * rinv**3).astype(BF16)
    partial_grad = mm_nt(query_grad, weights_all)
    modulated_grad = lax.psum_scatter(
        partial_grad.astype(BF16), "tp", scatter_dimension=1, tiled=True
    ).astype(F32)
    normed_grad = modulated_grad * (1.0 + scale_mod)
    grad_total, grad_cross = lax.psum(
        (jnp.sum(normed_grad, axis=1), jnp.sum(normed_grad * normed, axis=1)), "tp"
    )
    latent_grad = inverse * (
        normed_grad
        - (grad_total / full_width)[:, None]
        - normed * (grad_cross / full_width)[:, None]
    )
    latent_grad = latent_grad.astype(BF16)
    partial_three = mm_tn(token_two, latent_grad).astype(BF16)
    token_grad = mm_nt(latent_grad, w_section3).astype(BF16)
    stacked_grad = mm_tn(select, token_grad)
    two_grad = (stacked_grad * silu_slope(z_two)).astype(BF16)
    wide_two = mm_tn(stacked_one, two_grad)
    grad_two = sum(
        wide_two[4 * c_one * q : 4 * c_one * (q + 1), c_two * q : c_two * (q + 1)] for q in range(4)
    )
    one_grad = (mm_nt(two_grad, w_quad) * silu_slope(z_one)).astype(BF16)
    grad_one = fold_one(mm_tn(pose_in, one_grad), depth, c_one)
    packed = jnp.concatenate([grad_two.reshape(-1), grad_one.reshape(-1)])
    cut = grad_two.size
    if chips:
        padded = jnp.pad(packed, (0, -packed.size % 1024)).reshape(-1, 128)
        section_three_grad, packed = reduce_grads(partial_three, padded)
        packed = packed.reshape(-1)[: cut + grad_one.size]
    else:
        section_three_grad = lax.psum_scatter(partial_three, "seq", scatter_dimension=0, tiled=True).astype(F32)
        packed = lax.psum(packed, ("seq", "tp"))
    return (
        normed_query,
        section_three_grad,
        packed[:cut].reshape(grad_two.shape),
        packed[cut:].reshape(grad_one.shape),
    )


def solution(mesh):
    return jax.shard_map(
        body,
        mesh=mesh,
        in_specs=(
            P("seq", "tp"),
            P("seq", None),
            P("seq", None),
            P("seq"),
            P(),
            P(),
            P(None, "tp"),
            P("tp"),
            P("tp"),
            P("seq", "tp"),
            P("tp"),
            P("tp"),
            P("seq", "tp"),
        ),
        out_specs=(P("seq", "tp"), P("seq", "tp"), P(), P()),
        check_vma=False,
    )
```

```python
import jax
import jax.numpy as jnp
import numpy as np
from jax import lax
from jax.experimental import pallas as pl
from jax.experimental.pallas import tpu as pltpu
from jax.sharding import PartitionSpec as P

MESH = pl.DeviceIdType.MESH

epsilon = 1e-06
F32, BF16 = jnp.float32, jnp.bfloat16


def silu_slope(z):
    s = jax.nn.sigmoid(z)
    return s * (1.0 + z * (1.0 - s))


def mm(a, b):
    return jnp.dot(a, b, preferred_element_type=F32)


def mm_nt(a, b):
    return lax.dot_general(a, b, (((1,), (1,)), ((), ())), preferred_element_type=F32)


def mm_tn(a, b):
    return lax.dot_general(a, b, (((0,), (0,)), ((), ())), preferred_element_type=F32)


def cell_places():
    table = np.zeros((16, 16), np.float32)
    for i in range(4):
        for j in range(4):
            place = ((i // 2) * 2 + j // 2) * 4 + (i % 2) * 2 + j % 2
            table[4 * i + j, place] = 1.0
    return jnp.asarray(table)


def spread_one(w_one):
    depth, c_one = w_one.shape
    wide = cell_places()[:, None, :, None] * w_one.astype(F32)[None, :, None, :]
    return wide.reshape(16 * depth, 16 * c_one).astype(BF16)


def fold_one(wide, depth, c_one):
    blocks = wide.reshape(16, depth, 16, c_one) * cell_places()[:, None, :, None]
    return jnp.sum(blocks, axis=(0, 2))


def dispatch(pose_rows, dest_device, dest_slot, seq_count):
    count, width = pose_rows.shape
    capacity = max(2, 2 * count // seq_count)
    slots_all = seq_count * capacity
    owner = dest_device[:, 0]
    marks = (owner[:, None] == jnp.arange(seq_count, dtype=jnp.int32)[None, :]).astype(BF16)
    index = jnp.arange(count, dtype=jnp.int32)
    lower = (index[:, None] > index[None, :]).astype(BF16)
    before = mm(lower, marks)
    rank = jnp.sum(before * marks.astype(F32), axis=1).astype(jnp.int32)
    position = owner * capacity + rank
    place = (jnp.arange(slots_all, dtype=jnp.int32)[:, None] == position[None, :]).astype(BF16)
    lane = jnp.arange(128, dtype=jnp.int32)[None, :]
    slot = dest_slot[:, None]
    tail = jnp.where(lane == 0, slot // 128, jnp.where(lane == 1, slot % 128, jnp.where(lane == 2, 1, 0)))
    rows = jnp.concatenate([pose_rows, tail.astype(BF16)], axis=1)
    outgoing = mm(place, rows).astype(BF16)
    incoming = lax.all_to_all(
        outgoing.reshape(seq_count, capacity, width + 128), "seq", split_axis=0, concat_axis=0, tiled=True
    ).reshape(slots_all, width + 128)
    info = incoming[:, width : width + 3].astype(F32)
    slot_recv = (info[:, 0] * 128.0 + info[:, 1]).astype(jnp.int32)
    slot_recv = jnp.where(info[:, 2] > 0.5, slot_recv, -1)
    return incoming[:, :width], slot_recv


def place_here():
    me, core = lax.axis_index("seq"), lax.axis_index("tp")
    return me // 4, (me // 2) % 2, me % 2, core


def greet(devices, count):
    barrier = pltpu.get_barrier_semaphore()
    for condition, device in devices:

        def say(device=device):
            pl.semaphore_signal(barrier, inc=1, device_id=device, device_id_type=MESH)

        if condition is None:
            say()
        else:
            pl.when(condition)(say)
    pl.semaphore_wait(barrier, count)


def gather_kernel(w_ref, out_ref, own_sem, up_send, up_recv, down_send, down_recv, send_sem, recv_sem, cu_send, cu_recv, cd_send, cd_recv):
    z, y, x, core = place_here()
    third = w_ref.shape[0] // 80 * 16
    half = (w_ref.shape[0] - third) // 2
    rows_a, rows_b, rows_c = pl.ds(0, half), pl.ds(half, half), pl.ds(2 * half, third)
    rows_c1, rows_c2 = pl.ds(2 * half, third // 2), pl.ds(2 * half + third // 2, third // 2)
    last = 3

    def device(zz, yy, xx):
        return (zz * 4 + yy * 2 + xx, core)

    x_side, y_side = device(z, y, 1 - x), device(z, 1 - y, x)
    above, below = device(jnp.minimum(z + 1, last), y, x), device(jnp.maximum(z - 1, 0), y, x)
    greet(
        [(None, x_side), (None, y_side), (z < last, above), (z > 0, below)],
        2 + (z < last).astype(jnp.int32) + (z > 0).astype(jnp.int32),
    )

    def remote(src, dst, sems, target):
        return pltpu.make_async_remote_copy(
            src_ref=src, dst_ref=dst, send_sem=sems[0], recv_sem=sems[1], device_id=target, device_id_type=MESH
        )

    def line_copy(zz, step, up, src=None):
        block = out_ref.at[zz, y, x]
        send, recv = (up_send, up_recv) if up else (down_send, down_recv)
        return remote(block if src is None else src, block, (send.at[step], recv.at[step]), above if up else below)

    kinds = (
        (y, x, rows_a, True),
        (y, x, rows_b, False),
        (y, x, rows_a, False),
        (y, x, rows_b, True),
        (y, 1 - x, rows_a, False),
        (1 - y, x, rows_b, True),
        (y, x, rows_c, True),
        (y, x, rows_c, False),
        (y, 1 - x, rows_c1, False),
        (1 - y, x, rows_c2, True),
    )
    others = ((y, 1 - x), (1 - y, x), (1 - y, 1 - x))

    def thin_copy(spot, zz, step, up):
        block = out_ref.at[zz, others[spot][0], others[spot][1], rows_c]
        send, recv = (cu_send, cu_recv) if up else (cd_send, cd_recv)
        index = spot * 3 + step
        return remote(block, block, (send.at[index], recv.at[index]), above if up else below)

    def thin_start(spot):
        pl.when(z < last)(lambda: thin_copy(spot, z, 0, True).start())
        pl.when(z > 0)(lambda: thin_copy(spot, z, 0, False).start())

    def plane_copy(kind, zz, own=False):
        yy, xx, rows, to_x = kinds[kind]
        block = out_ref.at[zz, yy, xx, rows]
        return remote(
            w_ref.at[rows] if own else block,
            block,
            (send_sem.at[kind, zz], recv_sem.at[kind, zz]),
            x_side if to_x else y_side,
        )

    def arrival(kind, zz):
        yy, xx, rows, to_x = kinds[kind]
        yy, xx = (yy, 1 - xx) if to_x else (1 - yy, xx)
        block = out_ref.at[zz, yy, xx, rows]
        return remote(block, block, (send_sem.at[kind, zz], recv_sem.at[kind, zz]), x_side if to_x else y_side)

    def relay(zz):
        arrival(0, zz).wait_recv()
        plane_copy(4, zz).start()
        arrival(1, zz).wait_recv()
        plane_copy(5, zz).start()

    pl.when(z < last)(lambda: line_copy(z, 0, True, w_ref).start())
    pl.when(z > 0)(lambda: line_copy(z, 0, False, w_ref).start())
    for kind in (6, 7, 0, 1, 2, 3):
        plane_copy(kind, z, True).start()
    own = pltpu.make_async_copy(w_ref, out_ref.at[z, y, x], own_sem)
    own.start()
    for spot in range(2):
        arrival(6 + spot, z).wait_recv()
        plane_copy(8 + spot, z).start()
        thin_start(spot)
    arrival(8, z).wait_recv()
    arrival(9, z).wait_recv()
    thin_start(2)
    for step in range(1, 4):
        for up in (True, False):
            zz = z - step if up else z + step
            came = zz >= 0 if up else zz <= last
            goes_on = jnp.logical_and(came, z < last if up else z > 0)

            def arrive(zz=zz, step=step, up=up):
                line_copy(zz, step - 1, up).wait_recv()

            def pass_on(zz=zz, step=step, up=up):
                line_copy(zz, step, up).start()

            def spread(zz=zz):
                for kind in range(4):
                    plane_copy(kind, zz).start()

            pl.when(came)(arrive)
            if step < 3:
                pl.when(goes_on)(pass_on)
            pl.when(came)(spread)
        if step == 1:
            relay(z)
        else:
            for zz, came in ((z - step + 1, z - step + 1 >= 0), (z + step - 1, z + step - 1 <= last)):
                pl.when(came)(lambda zz=zz: relay(zz))
        for spot in range(3):
            for up in (True, False):
                zz = z - step if up else z + step
                came = zz >= 0 if up else zz <= last

                def thin_arrive(spot=spot, zz=zz, step=step, up=up):
                    thin_copy(spot, zz, step - 1, up).wait_recv()

                def thin_on(spot=spot, zz=zz, step=step, up=up):
                    thin_copy(spot, zz, step, up).start()

                pl.when(came)(thin_arrive)
                if step < 3:
                    pl.when(jnp.logical_and(came, z < last if up else z > 0))(thin_on)
    for zz, came in ((z - 3, z - 3 >= 0), (z + 3, z + 3 <= last)):
        pl.when(came)(lambda zz=zz: relay(zz))
    own.wait()
    for zz in range(4):
        for kind in range(2, 6):
            arrival(kind, zz).wait_recv()
        for kind in range(6):
            plane_copy(kind, zz).wait_send()
    for kind in range(6, 10):
        plane_copy(kind, z).wait_send()
    for step in range(3):
        for spot in range(3):
            pl.when(jnp.logical_and(z - step >= 0, z < last))(
                lambda step=step, spot=spot: thin_copy(spot, z - step, step, True).wait_send()
            )
            pl.when(jnp.logical_and(z + step <= last, z > 0))(
                lambda step=step, spot=spot: thin_copy(spot, z + step, step, False).wait_send()
            )
        pl.when(jnp.logical_and(z - step >= 0, z < last))(
            lambda step=step: line_copy(z - step, step, True).wait_send()
        )
        pl.when(jnp.logical_and(z + step <= last, z > 0))(
            lambda step=step: line_copy(z + step, step, False).wait_send()
        )


def gather_weights(w_query):
    depth, columns = w_query.shape
    dma = pltpu.SemaphoreType.DMA
    out = pl.pallas_call(
        gather_kernel,
        out_shape=jax.ShapeDtypeStruct((4, 2, 2, depth, columns), w_query.dtype),
        in_specs=[pl.BlockSpec(memory_space=pl.ANY)],
        out_specs=pl.BlockSpec(memory_space=pl.ANY),
        scratch_shapes=[dma, dma((3,)), dma((3,)), dma((3,)), dma((3,)), dma((10, 4)), dma((10, 4))] + [dma((9,))] * 4,
        compiler_params=pltpu.CompilerParams(collective_id=0, has_side_effects=True),
    )(w_query)
    return out.reshape(16 * depth, columns)


def reduce_kernel(
    p_ref, g_ref, out_ref, small_ref, one_a, one_b, sum_a, sum_b, two_a, two_b, line, line_in,
    small, small_in, small_z, send_sem, recv_sem, line_send, line_recv, g_send, g_recv, gz_send, gz_recv,
):
    z, y, x, core = place_here()
    half = p_ref.shape[-1] // 2
    cols_a, cols_b = pl.ds(0, half), pl.ds(half, half)

    def device(zz, yy, xx, cc):
        return (zz * 4 + yy * 2 + xx, cc)

    x_side, y_side, core_side = device(z, y, 1 - x, core), device(z, 1 - y, x, core), device(z, y, x, 1 - core)
    peers = [lax.rem(z + d, 4) for d in (1, 2, 3)]
    greet([(None, t) for t in [x_side, y_side, core_side] + [device(p, y, x, core) for p in peers]], 6)

    def send(src, dst, sems, target):
        copy = pltpu.make_async_remote_copy(
            src_ref=src, dst_ref=dst, send_sem=sems[0], recv_sem=sems[1], device_id=target, device_id_type=MESH
        )
        copy.start()
        return copy

    def sems(i):
        return (send_sem.at[i], recv_sem.at[i])

    def added(a, b):
        return (a.astype(F32) + b.astype(F32)).astype(BF16)

    first_a = send(p_ref.at[:, :, 1 - x, :, cols_a], one_a, sems(0), x_side)
    first_b = send(p_ref.at[:, 1 - y, :, :, cols_b], one_b, sems(1), y_side)
    small[0] = g_ref[...]
    for i, target in enumerate((core_side, x_side, y_side)):
        send(small.at[i], small_in.at[i], (g_send.at[i], g_recv.at[i]), target).wait()
        small[i + 1] = small[i] + small_in[i]
    small_z[z] = small[3]
    g_line = [
        send(small.at[3], small_z.at[z], (gz_send.at[d], gz_recv.at[d]), device(peers[d], y, x, core))
        for d in range(3)
    ]
    first_a.wait()
    for zz in range(4):
        for q in range(2):
            sum_a[zz, q] = added(p_ref[zz, q, x, :, 0:half], one_a[zz, q])
    second_a = send(sum_a.at[:, 1 - y], two_a, sems(2), y_side)
    first_b.wait()
    for zz in range(4):
        for q in range(2):
            sum_b[zz, q] = added(p_ref[zz, y, q, :, half:], one_b[zz, q])
    second_b = send(sum_b.at[:, 1 - x], two_b, sems(3), x_side)
    second_a.wait()
    for zz in range(4):
        line[zz, :, 0:half] = added(sum_a[zz, y], two_a[zz])
    second_b.wait()
    for zz in range(4):
        line[zz, :, half:] = added(sum_b[zz, x], two_b[zz])
    last = [
        send(line.at[peers[d]], line_in.at[d], (line_send.at[d], line_recv.at[d]), device(peers[d], y, x, core))
        for d in range(3)
    ]
    for copy in g_line:
        copy.wait()
    small_ref[...] = (small_z[0] + small_z[1]) + (small_z[2] + small_z[3])
    for copy in last:
        copy.wait()
    total = line[z].astype(F32)
    for d in range(3):
        total = total + line_in[d].astype(F32)
    out_ref[...] = total


def reduce_grads(partial, small):
    rows, columns = partial.shape
    piece, half = rows // 16, columns // 2
    dma = pltpu.SemaphoreType.DMA
    vmem = pl.BlockSpec(memory_space=pltpu.VMEM)
    return pl.pallas_call(
        reduce_kernel,
        out_shape=(jax.ShapeDtypeStruct((piece, columns), F32), jax.ShapeDtypeStruct(small.shape, F32)),
        in_specs=[vmem, vmem],
        out_specs=(vmem, vmem),
        scratch_shapes=[pltpu.VMEM((4, 2, piece, half), BF16)] * 4
        + [pltpu.VMEM((4, piece, half), BF16)] * 2
        + [pltpu.VMEM((4, piece, columns), BF16), pltpu.VMEM((3, piece, columns), BF16)]
        + [pltpu.VMEM((4,) + small.shape, F32), pltpu.VMEM((3,) + small.shape, F32), pltpu.VMEM((4,) + small.shape, F32)]
        + [dma((4,)), dma((4,)), dma((3,)), dma((3,)), dma((3,)), dma((3,)), dma((3,)), dma((3,))],
        compiler_params=pltpu.CompilerParams(collective_id=1, has_side_effects=True, vmem_limit_bytes=32 << 20),
    )(partial.reshape(4, 2, 2, piece, columns), small)


def body(
    latent,
    pose_rows,
    dest_device,
    dest_slot,
    w_section1,
    w_section2,
    w_section3,
    shift_mod,
    scale_mod,
    w_query,
    bias_query,
    gain_query,
    cotangent,
):
    tokens = latent.shape[0]
    seq_count = lax.axis_size("seq")
    tp_count = lax.axis_size("tp")
    full_width = latent.shape[1] * tp_count
    query_width = w_query.shape[1] * tp_count
    depth, c_one = w_section1.shape
    c_two = w_section2.shape[1]
    chips = seq_count == 16 and tp_count == 2
    if chips:
        weights_all = gather_weights(w_query)
    else:
        weights_all = lax.all_gather(w_query, "seq", axis=0, tiled=True)
    pose_in, slot_recv = dispatch(pose_rows, dest_device, dest_slot, seq_count)
    w_wide = spread_one(w_section1)
    w_quad = jnp.kron(jnp.eye(4, dtype=BF16), w_section2)
    z_one = mm(pose_in, w_wide)
    stacked_one = jax.nn.silu(z_one).astype(BF16)
    z_two = mm(stacked_one, w_quad)
    stacked_two = jax.nn.silu(z_two).astype(BF16)
    select = (jnp.arange(tokens, dtype=jnp.int32)[:, None] == slot_recv[None, :]).astype(BF16)
    token_two = mm(select, stacked_two).astype(BF16)
    guidance = mm(token_two, w_section3)
    summed = latent.astype(F32) + guidance
    total, squares = lax.psum((jnp.sum(summed, axis=1), jnp.sum(summed * summed, axis=1)), "tp")
    center = total / full_width
    inverse = lax.rsqrt(squares / full_width - center * center + epsilon)[:, None]
    normed = (summed - center[:, None]) * inverse
    modulated = (normed * (1.0 + scale_mod) + shift_mod).astype(BF16)
    whole = lax.all_gather(modulated, "tp", axis=1, tiled=True)
    query = mm(whole, weights_all) + bias_query
    upstream = cotangent.astype(F32) * gain_query
    sum_square, sum_along = lax.psum(
        (jnp.sum(query * query, axis=1), jnp.sum(upstream * query, axis=1)), "tp"
    )
    rinv = lax.rsqrt(sum_square / query_width + epsilon)[:, None]
    normed_query = (query * rinv * gain_query).astype(BF16)
    along = (sum_along / query_width)[:, None]
    query_grad = (upstream * rinv - query * along * rinv**3).astype(BF16)
    partial_grad = mm_nt(query_grad, weights_all)
    modulated_grad = lax.psum_scatter(
        partial_grad.astype(BF16), "tp", scatter_dimension=1, tiled=True
    ).astype(F32)
    normed_grad = modulated_grad * (1.0 + scale_mod)
    grad_total, grad_cross = lax.psum(
        (jnp.sum(normed_grad, axis=1), jnp.sum(normed_grad * normed, axis=1)), "tp"
    )
    latent_grad = inverse * (
        normed_grad
        - (grad_total / full_width)[:, None]
        - normed * (grad_cross / full_width)[:, None]
    )
    latent_grad = latent_grad.astype(BF16)
    partial_three = mm_tn(token_two, latent_grad).astype(BF16)
    token_grad = mm_nt(latent_grad, w_section3).astype(BF16)
    stacked_grad = mm_tn(select, token_grad)
    two_grad = (stacked_grad * silu_slope(z_two)).astype(BF16)
    wide_two = mm_tn(stacked_one, two_grad)
    grad_two = sum(
        wide_two[4 * c_one * q : 4 * c_one * (q + 1), c_two * q : c_two * (q + 1)] for q in range(4)
    )
    one_grad = (mm_nt(two_grad, w_quad) * silu_slope(z_one)).astype(BF16)
    grad_one = fold_one(mm_tn(pose_in, one_grad), depth, c_one)
    packed = jnp.concatenate([grad_two.reshape(-1), grad_one.reshape(-1)])
    cut = grad_two.size
    if chips:
        padded = jnp.pad(packed, (0, -packed.size % 1024)).reshape(-1, 128)
        section_three_grad, packed = reduce_grads(partial_three, padded)
        packed = packed.reshape(-1)[: cut + grad_one.size]
    else:
        section_three_grad = lax.psum_scatter(partial_three, "seq", scatter_dimension=0, tiled=True).astype(F32)
        packed = lax.psum(packed, ("seq", "tp"))
    return (
        normed_query,
        section_three_grad,
        packed[:cut].reshape(grad_two.shape),
        packed[cut:].reshape(grad_one.shape),
    )


def solution(mesh):
    return jax.shard_map(
        body,
        mesh=mesh,
        in_specs=(
            P("seq", "tp"),
            P("seq", None),
            P("seq", None),
            P("seq"),
            P(),
            P(),
            P(None, "tp"),
            P("tp"),
            P("tp"),
            P("seq", "tp"),
            P("tp"),
            P("tp"),
            P("seq", "tp"),
        ),
        out_specs=(P("seq", "tp"), P("seq", "tp"), P(), P()),
        check_vma=False,
    )
```
